32 devices in a mesh: kloop: 16 (over z, y, x), pair: 2 (over core).
Axes of the slice: x: 2, y: 2, z: 4, core: 2. Of those that a mesh axis runs over, the one named last changes fastest.
Arguments:
- orbitals: bfloat16 [32, 32, 512], P('kloop'), may hold values from -6 to 6
- fitting: bfloat16 [512, 1400], replicated, may hold values from -0.25 to 0.25
- screen: bfloat16 [4, 1400, 1400], P(None, None, 'pair'), may hold values from -0.00390625 to 0.00390625
- coulomb: float32 [1400], replicated, may hold values from 0.005 to 0.1
- qindex: int32 [32, 2], replicated, may hold values from 0 to 3
Outputs:
- kernel: bfloat16 [32, 2, 256, 256], P('kloop', None, 'pair')
The draws below stay inside these ranges and needn't reach their ends.
Inputs may be any that keep to these rules, and one draw needn't show every extreme that they name: `qindex`: the index of the held screened interaction for each block.
All inputs are finite; a program needn't handle non-finite values.
Results may differ from the reference program's by a relative error of at most 0.0085.
Values may be sent and summed in bfloat16 or wider, within the bound.
A program may use at most 64 MiB of HBM per device.

```python
import math
import jax
import jax.numpy as jnp
from jax import lax

NV = 16
NC = 16
NB = 32
NG = 1400
MU = 512
NQ = 4
S = 2
K_DEV = 2
K = 32
N_KLOOP = 16
N_PAIR = 2


def with_ends(drawn, own_key, least, high):
    longest = drawn.shape.index(max(drawn.shape))
    spots = []
    for shift in (0, 1):
        where = [jax.random.randint(jax.random.fold_in(own_key, axis), (), 0, length) for axis, length in enumerate(drawn.shape)]
        where[longest] = (where[longest] + shift) % drawn.shape[longest]
        spots.append(tuple(where))
    return drawn.at[spots[0]].set(least).at[spots[1]].set(high)


def steps_of(key, extent, cuts, smallest, largest):
    gain, own = 1.0, jax.random.fold_in(key, 6)
    for position, blocks in cuts:
        heights = jnp.exp(jax.random.uniform(jax.random.fold_in(own, position), (blocks,), jnp.float32, smallest / len(cuts), largest / len(cuts)))
        gain = gain * jnp.repeat(heights, extent[position] // blocks).reshape([-1 if axis == position else 1 for axis in range(len(extent))])
    return gain


def bell_draw(rng, extent, width, limit, shards=(), held_as=jnp.bfloat16):
    values = jax.random.normal(rng, extent, jnp.float32) * width
    if len(shards) > 0:
        values = steps_of(rng, extent, shards, -0.22, 0.18) * values
    return jnp.clip(values, min=-limit, max=limit).astype(held_as)


def setup_inputs(seed: int = 0) -> dict:
    splits = jax.random.split(jax.random.key(seed), 6)
    orbitals = bell_draw(splits[0], (K, NB, MU), 1.0, 6.0, ((0, 16),))
    fitting = bell_draw(splits[1], (MU, NG), MU ** -0.5, 0.25)
    screen = bell_draw(splits[2], (NQ, NG, NG), (NG * NG) ** -0.5, 0.00390625, ((2, 2),))
    coulomb = jnp.clip(jnp.exp(jax.random.uniform(splits[3], (NG,), jnp.float32, math.log(0.005), math.log(0.1))), 0.005, 0.1)
    qindex = with_ends(jax.random.randint(splits[4], (K, S), 0, NQ), jax.random.fold_in(splits[4], 1), 0, NQ - 1).astype(jnp.int32)
    return {"orbitals": orbitals, "fitting": fitting, "screen": screen, "coulomb": coulomb, "qindex": qindex}


def pair_fields(left_bands, right_bands, fitting):
    products = (left_bands.astype(jnp.float32)[:, None, :] * right_bands.astype(jnp.float32)[None, :, :]).astype(jnp.bfloat16)
    flat = products.reshape(left_bands.shape[0] * right_bands.shape[0], left_bands.shape[1])
    return jnp.dot(flat, fitting, preferred_element_type=jnp.float32).astype(jnp.bfloat16)


def reference(orbitals, fitting, screen, coulomb, qindex):
    kpoints_all = K_DEV * N_KLOOP
    slice_width = NG // N_PAIR

    def own_fields(orbital):
        fields = pair_fields(orbital[:NV], orbital[NV:], fitting)
        weighted = (fields.astype(jnp.float32) * coulomb).astype(jnp.bfloat16)
        return fields, weighted

    own_all, weighted_all = lax.map(own_fields, orbitals)
    results = []
    for shift_step in range(1, S + 1):
        def one_block(column):
            row = (column + shift_step * K_DEV) % kpoints_all
            row_orb = orbitals[row]
            col_orb = orbitals[column]
            cond = pair_fields(row_orb[NV:], col_orb[NV:], fitting)
            vale = pair_fields(row_orb[:NV], col_orb[:NV], fitting)
            interaction = screen[qindex[column, shift_step - 1]]
            screened = jnp.dot(cond, interaction, preferred_element_type=jnp.float32).astype(jnp.bfloat16)
            cond_four = screened.astype(jnp.float32).reshape(NC, NC, N_PAIR, slice_width)
            vale_four = vale.astype(jnp.float32).reshape(NV, NV, N_PAIR, slice_width)
            parts = jnp.einsum("xypg,vwpg->pvxwy", cond_four, vale_four).reshape(N_PAIR, NV * NC, NV * NC)
            parts = lax.optimization_barrier(parts.astype(jnp.bfloat16)).astype(jnp.float32)
            direct = jnp.sum(parts, axis=0)
            exchange = lax.dot_general(weighted_all[row], own_all[column], (((1,), (1,)), ((), ())), preferred_element_type=jnp.float32)
            return (2.0 * exchange - direct).astype(jnp.bfloat16)

        results.append(lax.map(one_block, jnp.arange(kpoints_all, dtype=jnp.int32)))
    return jnp.stack(results, axis=1)
```

```python
import functools
import jax
import jax.numpy as jnp
from jax import lax
from jax.experimental import pallas as pl
from jax.experimental.pallas import tpu as pltpu
from jax.sharding import PartitionSpec as P

NV = 16
NC = 16
S = 2
LANES = 128
MESH = pl.DeviceIdType.MESH
NT = (((1,), (1,)), ((), ()))


def dot(left, right):
    return jnp.dot(left, right, preferred_element_type=jnp.float32)


def dot_nt(left, right):
    return lax.dot_general(left, right, NT, preferred_element_type=jnp.float32)


def products(major, minor):
    both = major[:, None, :] * minor[None, :, :]
    return both.astype(jnp.bfloat16).reshape(major.shape[0] * minor.shape[0], major.shape[1])


def chunks_of(width, n_q):
    for count in (5, 7, 4, 3, 2):
        if width % count == 0 and width // count * n_q % 16 == 0:
            return count
    return 1


def exchange_digits(value):
    lane = lax.broadcasted_iota(jnp.int32, (16, LANES), 1)
    halves = []
    for half in range(value.shape[1] // LANES):
        groups = [
            value[16 * g : 16 * g + 16, half * LANES : (half + 1) * LANES] for g in range(16)
        ]
        for bit in range(4):
            step = 1 << bit
            odd = (lane // step) % 2 == 1
            later = list(groups)
            for g in range(16):
                if g & step == 0:
                    low, high = groups[g], groups[g + step]
                    later[g] = jnp.where(odd, pltpu.roll(high, step, 1), low)
                    later[g + step] = jnp.where(odd, high, pltpu.roll(low, LANES - step, 1))
            groups = later
        halves.append(jnp.concatenate(groups, axis=0))
    return jnp.concatenate(halves, axis=1)


def body(
    loop_count,
    pair_count,
    orb_ref,
    coul_ref,
    q_ref,
    fit_hbm,
    screen_hbm,
    out_ref,
    fit,
    screen,
    fit_own,
    mixed,
    between,
    turned,
    arrived,
    part,
    leaving,
    landed,
    fit_sem,
    screen_sem,
    orb_send,
    orb_recv,
    part_send,
    part_recv,
):
    per_dev = orb_ref.shape[0]
    width, n_q, n_g = screen.shape
    rows = NV * NC // pair_count
    me = lax.axis_index("kloop")
    side = lax.axis_index("pair")
    chunks = chunks_of(width, n_q)
    chunk = width // chunks

    def fetch(index):
        span = pl.ds(index * chunk, chunk)
        return pltpu.make_async_copy(screen_hbm.at[span], screen.at[span], screen_sem.at[index])

    fit_copy = pltpu.make_async_copy(fit_hbm, fit, fit_sem)
    fit_copy.start()
    for index in range(chunks):
        fetch(index).start()

    barrier = pltpu.get_barrier_semaphore()
    for shift in range(1, S + 1):
        source = lax.rem(me + shift, loop_count)
        pl.semaphore_signal(barrier, inc=1, device_id={"kloop": source}, device_id_type=MESH)
    for offset in range(1, pair_count):
        other = lax.rem(side + offset, pair_count)
        pl.semaphore_signal(barrier, inc=1, device_id={"pair": other}, device_id_type=MESH)

    fit_copy.wait()
    for index in range(pair_count):

        @pl.when(side == index)
        def _():
            own = fit[index * width : (index + 1) * width, :]
            across = own.T
            fit_own[...] = across
            weight = coul_ref[:, index * width : (index + 1) * width]
            weighted = (across.astype(jnp.float32) * weight).astype(jnp.bfloat16)
            coupling = dot(weighted, own).astype(jnp.bfloat16)
            for k in range(per_dev):
                orb = orb_ref[k].astype(jnp.float32)
                turned[k] = dot(products(orb[:NV], orb[NV:]), coupling).astype(jnp.bfloat16)

    pl.semaphore_wait(barrier, S + pair_count - 1)
    orb_copies = []
    for shift in range(1, S + 1):
        target = lax.rem(me - shift + loop_count, loop_count)
        orb_copies.append(
            pltpu.make_async_remote_copy(
                src_ref=orb_ref,
                dst_ref=arrived.at[shift - 1],
                send_sem=orb_send.at[shift - 1],
                recv_sem=orb_recv.at[shift - 1],
                device_id={"kloop": target},
                device_id_type=MESH,
            )
        )
        orb_copies[-1].start()

    @pl.loop(0, chunks)
    def _(index):
        fetch(index).wait()
        taken = screen[pl.ds(index * chunk, chunk)].reshape(chunk * n_q, n_g)
        start = pl.multiple_of(index * chunk * n_q, 8)
        result = dot(taken, fit[...])
        for tile in range(result.shape[1] // LANES):
            mixed[tile, pl.ds(start, chunk * n_q), :] = result[:, tile * LANES : (tile + 1) * LANES]

    for q in range(n_q):
        half = jnp.concatenate(
            [mixed[tile, pl.ds(q, width, stride=n_q), :] for tile in range(mixed.shape[0])], axis=1
        )
        between[q] = dot(fit_own[...], half.astype(jnp.bfloat16)).astype(jnp.bfloat16)

    part_copies = []
    for shift in range(1, S + 1):
        orb_copies[shift - 1].wait()
        for k in range(per_dev):
            block = (shift - 1) * per_dev + k
            row = arrived[shift - 1, k].astype(jnp.float32)
            col = orb_ref[k].astype(jnp.float32)
            q = q_ref[shift - 1, me * per_dev + k]
            cond = products(col[NV:], row[NV:])
            screened = dot_nt(cond, between[q]).astype(jnp.bfloat16)
            direct = exchange_digits(dot_nt(screened, products(col[:NV], row[:NV])))
            exchange = dot_nt(products(row[:NV], row[NV:]), turned[k])
            total = 2.0 * exchange - direct
            part[block] = total
            leaving[block] = total.astype(jnp.bfloat16)
            for offset in range(1, pair_count):
                other = lax.rem(side + offset, pair_count)
                copy = pltpu.make_async_remote_copy(
                    src_ref=leaving.at[block, pl.ds(pl.multiple_of(other * rows, rows), rows)],
                    dst_ref=landed.at[block, offset - 1],
                    send_sem=part_send.at[block, offset - 1],
                    recv_sem=part_recv.at[block, offset - 1],
                    device_id={"pair": other},
                    device_id_type=MESH,
                )
                copy.start()
                part_copies.append(copy)

    for shift in range(1, S + 1):
        for k in range(per_dev):
            block = (shift - 1) * per_dev + k
            total = part[block, pl.ds(pl.multiple_of(side * rows, rows), rows), :]
            for offset in range(1, pair_count):
                part_copies[block * (pair_count - 1) + offset - 1].wait()
                total = total + landed[block, offset - 1].astype(jnp.float32)
            out_ref[k, shift - 1] = total.astype(jnp.bfloat16)


def shards(orbitals, fitting, screen, coulomb, qindex):
    per_dev, bands, points = orbitals.shape
    pair_count = lax.axis_size("pair")
    loop_count = lax.axis_size("kloop")
    n_q, n_g, width = screen.shape
    rows = NV * NC // pair_count
    blocks = S * per_dev
    n = NV * NC
    flops = 2 * n_q * points * width * (n_g + points) + 2 * points * points * width
    flops += blocks * 2 * n * points * (points + 2 * n)
    vmem = pl.BlockSpec(memory_space=pltpu.VMEM)
    dma = pltpu.SemaphoreType.DMA
    return pl.pallas_call(
        functools.partial(body, loop_count, pair_count),
        out_shape=jax.ShapeDtypeStruct((per_dev, S, rows, n), jnp.bfloat16),
        in_specs=[
            vmem,
            vmem,
            pl.BlockSpec(memory_space=pltpu.SMEM),
            pl.BlockSpec(memory_space=pl.ANY),
            pl.BlockSpec(memory_space=pl.ANY),
        ],
        out_specs=vmem,
        scratch_shapes=[
            pltpu.VMEM((n_g, points), jnp.bfloat16),
            pltpu.VMEM((width, n_q, n_g), jnp.bfloat16),
            pltpu.VMEM((points, width), jnp.bfloat16),
            pltpu.VMEM((points // LANES, width * n_q, LANES), jnp.float32),
            pltpu.VMEM((n_q, points, points), jnp.bfloat16),
            pltpu.VMEM((per_dev, n, points), jnp.bfloat16),
            pltpu.VMEM((S, per_dev, bands, points), jnp.bfloat16),
            pltpu.VMEM((blocks, n, n), jnp.float32),
            pltpu.VMEM((blocks, n, n), jnp.bfloat16),
            pltpu.VMEM((blocks, max(pair_count - 1, 1), rows, n), jnp.bfloat16),
            dma,
            dma((chunks_of(width, n_q),)),
            dma((S,)),
            dma((S,)),
            dma((blocks, max(pair_count - 1, 1))),
            dma((blocks, max(pair_count - 1, 1))),
        ],
        compiler_params=pltpu.CompilerParams(
            collective_id=0, has_side_effects=True, vmem_limit_bytes=52 * 1024 * 1024
        ),
        cost_estimate=pl.CostEstimate(
            flops=flops, bytes_accessed=2 * (n_q * n_g * width + points * n_g), transcendentals=0
        ),
    )(orbitals, coulomb.reshape(1, n_g), qindex.T, fitting.T, jnp.transpose(screen, (2, 0, 1)))


def solution(mesh):
    return jax.shard_map(
        shards,
        mesh=mesh,
        in_specs=(P("kloop", None, None), P(), P(None, None, "pair"), P(), P()),
        out_specs=P("kloop", None, "pair", None),
        check_vma=False,
    )
```

```python
import functools
import jax
import jax.numpy as jnp
from jax import lax
from jax.experimental import pallas as pl
from jax.experimental.pallas import tpu as pltpu
from jax.sharding import PartitionSpec as P

NV = 16
NC = 16
S = 2
LANES = 128
MESH = pl.DeviceIdType.MESH
NT = (((1,), (1,)), ((), ()))


def dot(left, right):
    return jnp.dot(left, right, preferred_element_type=jnp.float32)


def dot_nt(left, right):
    return lax.dot_general(left, right, NT, preferred_element_type=jnp.float32)


def products(major, minor):
    both = major[:, None, :] * minor[None, :, :]
    return both.astype(jnp.bfloat16).reshape(major.shape[0] * minor.shape[0], major.shape[1])


def chunks_of(width, n_q):
    for count in (5, 7, 4, 3, 2):
        if width % count == 0 and width // count * n_q % 16 == 0:
            return count
    return 1


def exchange_digits(value):
    lane = lax.broadcasted_iota(jnp.int32, (16, LANES), 1)
    halves = []
    for half in range(value.shape[1] // LANES):
        groups = [
            value[16 * g : 16 * g + 16, half * LANES : (half + 1) * LANES] for g in range(16)
        ]
        for bit in range(4):
            step = 1 << bit
            odd = (lane // step) % 2 == 1
            later = list(groups)
            for g in range(16):
                if g & step == 0:
                    low, high = groups[g], groups[g + step]
                    later[g] = jnp.where(odd, pltpu.roll(high, step, 1), low)
                    later[g + step] = jnp.where(odd, high, pltpu.roll(low, LANES - step, 1))
            groups = later
        halves.append(jnp.concatenate(groups, axis=0))
    return jnp.concatenate(halves, axis=1)


def body(
    loop_count,
    pair_count,
    orb_hbm,
    coul_hbm,
    q_hbm,
    fit_hbm,
    screen_hbm,
    out_ref,
    orb_ref,
    coul_ref,
    q_ref,
    fit,
    screen,
    fit_own,
    mixed,
    between,
    turned,
    arrived,
    part,
    leaving,
    landed,
    orb_sem,
    coul_sem,
    q_sem,
    fit_sem,
    screen_sem,
    orb_send,
    orb_recv,
    part_send,
    part_recv,
):
    per_dev = orb_ref.shape[0]
    width, n_q, n_g = screen.shape
    rows = NV * NC // pair_count
    me = lax.axis_index("kloop")
    side = lax.axis_index("pair")
    chunks = chunks_of(width, n_q)
    chunk = width // chunks

    def fetch(index):
        span = pl.ds(index * chunk, chunk)
        return pltpu.make_async_copy(screen_hbm.at[span], screen.at[span], screen_sem.at[index])

    fit_copy = pltpu.make_async_copy(fit_hbm, fit, fit_sem)
    orb_copy = pltpu.make_async_copy(orb_hbm, orb_ref, orb_sem)
    coul_copy = pltpu.make_async_copy(coul_hbm, coul_ref, coul_sem)
    q_copy = pltpu.make_async_copy(q_hbm, q_ref, q_sem)
    for copy in (orb_copy, coul_copy, q_copy, fit_copy):
        copy.start()
    for index in range(chunks):
        fetch(index).start()

    barrier = pltpu.get_barrier_semaphore()
    for shift in range(1, S + 1):
        source = lax.rem(me + shift, loop_count)
        pl.semaphore_signal(barrier, inc=1, device_id={"kloop": source}, device_id_type=MESH)
    for offset in range(1, pair_count):
        other = lax.rem(side + offset, pair_count)
        pl.semaphore_signal(barrier, inc=1, device_id={"pair": other}, device_id_type=MESH)

    for copy in (orb_copy, coul_copy, q_copy, fit_copy):
        copy.wait()
    all_weights = coul_ref[...].reshape(1, n_g)
    for index in range(pair_count):

        @pl.when(side == index)
        def _():
            own = fit[index * width : (index + 1) * width, :]
            across = own.T
            fit_own[...] = across
            weight = all_weights[:, index * width : (index + 1) * width]
            weighted = (across.astype(jnp.float32) * weight).astype(jnp.bfloat16)
            coupling = dot(weighted, own).astype(jnp.bfloat16)
            for k in range(per_dev):
                orb = orb_ref[k].astype(jnp.float32)
                turned[k] = dot(products(orb[:NV], orb[NV:]), coupling).astype(jnp.bfloat16)

    pl.semaphore_wait(barrier, S + pair_count - 1)
    orb_copies = []
    for shift in range(1, S + 1):
        target = lax.rem(me - shift + loop_count, loop_count)
        orb_copies.append(
            pltpu.make_async_remote_copy(
                src_ref=orb_ref,
                dst_ref=arrived.at[shift - 1],
                send_sem=orb_send.at[shift - 1],
                recv_sem=orb_recv.at[shift - 1],
                device_id={"kloop": target},
                device_id_type=MESH,
            )
        )
        orb_copies[-1].start()

    @pl.loop(0, chunks)
    def _(index):
        fetch(index).wait()
        taken = screen[pl.ds(index * chunk, chunk)].reshape(chunk * n_q, n_g)
        start = pl.multiple_of(index * chunk * n_q, 8)
        result = dot(taken, fit[...])
        for tile in range(result.shape[1] // LANES):
            mixed[tile, pl.ds(start, chunk * n_q), :] = result[:, tile * LANES : (tile + 1) * LANES]

    for q in range(n_q):
        half = jnp.concatenate(
            [mixed[tile, pl.ds(q, width, stride=n_q), :] for tile in range(mixed.shape[0])], axis=1
        )
        between[q] = dot(fit_own[...], half.astype(jnp.bfloat16)).astype(jnp.bfloat16)

    part_copies = []
    for shift in range(1, S + 1):
        orb_copies[shift - 1].wait()
        for k in range(per_dev):
            block = (shift - 1) * per_dev + k
            row = arrived[shift - 1, k].astype(jnp.float32)
            col = orb_ref[k].astype(jnp.float32)
            q = q_ref[shift - 1, me * per_dev + k]
            cond = products(col[NV:], row[NV:])
            screened = dot_nt(cond, between[q]).astype(jnp.bfloat16)
            direct = exchange_digits(dot_nt(screened, products(col[:NV], row[:NV])))
            exchange = dot_nt(products(row[:NV], row[NV:]), turned[k])
            total = 2.0 * exchange - direct
            part[block] = total
            leaving[block] = total.astype(jnp.bfloat16)
            for offset in range(1, pair_count):
                other = lax.rem(side + offset, pair_count)
                copy = pltpu.make_async_remote_copy(
                    src_ref=leaving.at[block, pl.ds(pl.multiple_of(other * rows, rows), rows)],
                    dst_ref=landed.at[block, offset - 1],
                    send_sem=part_send.at[block, offset - 1],
                    recv_sem=part_recv.at[block, offset - 1],
                    device_id={"pair": other},
                    device_id_type=MESH,
                )
                copy.start()
                part_copies.append(copy)

    for shift in range(1, S + 1):
        for k in range(per_dev):
            block = (shift - 1) * per_dev + k
            total = part[block, pl.ds(pl.multiple_of(side * rows, rows), rows), :]
            for offset in range(1, pair_count):
                part_copies[block * (pair_count - 1) + offset - 1].wait()
                total = total + landed[block, offset - 1].astype(jnp.float32)
            out_ref[k, shift - 1] = total.astype(jnp.bfloat16)


def shards(orbitals, fitting, screen, coulomb, qindex):
    per_dev, bands, points = orbitals.shape
    pair_count = lax.axis_size("pair")
    loop_count = lax.axis_size("kloop")
    n_q, n_g, width = screen.shape
    rows = NV * NC // pair_count
    blocks = S * per_dev
    n = NV * NC
    flops = 2 * n_q * points * width * (n_g + points) + 2 * points * points * width
    flops += blocks * 2 * n * points * (points + 2 * n)
    vmem = pl.BlockSpec(memory_space=pltpu.VMEM)
    dma = pltpu.SemaphoreType.DMA
    return pl.pallas_call(
        functools.partial(body, loop_count, pair_count),
        out_shape=jax.ShapeDtypeStruct((per_dev, S, rows, n), jnp.bfloat16),
        in_specs=[
            pl.BlockSpec(memory_space=pltpu.HBM),
            pl.BlockSpec(memory_space=pltpu.HBM),
            pl.BlockSpec(memory_space=pltpu.HBM),
            pl.BlockSpec(memory_space=pltpu.HBM),
            pl.BlockSpec(memory_space=pltpu.HBM),
        ],
        out_specs=vmem,
        scratch_shapes=[
            pltpu.VMEM((per_dev, bands, points), jnp.bfloat16),
            pltpu.VMEM((n_g,), jnp.float32),
            pltpu.SMEM((S, per_dev * loop_count), jnp.int32),
            pltpu.VMEM((n_g, points), jnp.bfloat16),
            pltpu.VMEM((width, n_q, n_g), jnp.bfloat16),
            pltpu.VMEM((points, width), jnp.bfloat16),
            pltpu.VMEM((points // LANES, width * n_q, LANES), jnp.float32),
            pltpu.VMEM((n_q, points, points), jnp.bfloat16),
            pltpu.VMEM((per_dev, n, points), jnp.bfloat16),
            pltpu.VMEM((S, per_dev, bands, points), jnp.bfloat16),
            pltpu.VMEM((blocks, n, n), jnp.float32),
            pltpu.VMEM((blocks, n, n), jnp.bfloat16),
            pltpu.VMEM((blocks, max(pair_count - 1, 1), rows, n), jnp.bfloat16),
            dma,
            dma,
            dma,
            dma,
            dma((chunks_of(width, n_q),)),
            dma((S,)),
            dma((S,)),
            dma((blocks, max(pair_count - 1, 1))),
            dma((blocks, max(pair_count - 1, 1))),
        ],
        compiler_params=pltpu.CompilerParams(
            collective_id=0, has_side_effects=True, vmem_limit_bytes=64 * 1024 * 1024
        ),
        cost_estimate=pl.CostEstimate(
            flops=flops, bytes_accessed=2 * (n_q * n_g * width + points * n_g), transcendentals=0
        ),
    )(orbitals, coulomb, qindex.T, fitting.T, jnp.transpose(screen, (2, 0, 1)))


def solution(mesh):
    return jax.shard_map(
        shards,
        mesh=mesh,
        in_specs=(P("kloop", None, None), P(), P(None, None, "pair"), P(), P()),
        out_specs=P("kloop", None, "pair", None),
        check_vma=False,
    )
```

```python
import functools
import jax
import jax.numpy as jnp
from jax import lax
from jax.experimental import pallas as pl
from jax.experimental.pallas import tpu as pltpu
from jax.sharding import PartitionSpec as P

NV = 16
NC = 16
S = 2
LANES = 128
MESH = pl.DeviceIdType.MESH
NT = (((1,), (1,)), ((), ()))


def dot(left, right):
    return jnp.dot(left, right, preferred_element_type=jnp.float32)


def dot_nt(left, right):
    return lax.dot_general(left, right, NT, preferred_element_type=jnp.float32)


def products(major, minor):
    both = major[:, None, :] * minor[None, :, :]
    return both.astype(jnp.bfloat16).reshape(major.shape[0] * minor.shape[0], major.shape[1])


def chunks_of(width, n_q):
    for count in (5, 7, 4, 3, 2):
        if width % count == 0 and width // count * n_q % 16 == 0:
            return count
    return 1


def exchange_digits(value):
    lane = lax.broadcasted_iota(jnp.int32, (16, LANES), 1)
    halves = []
    for half in range(value.shape[1] // LANES):
        groups = [
            value[16 * g : 16 * g + 16, half * LANES : (half + 1) * LANES] for g in range(16)
        ]
        for bit in range(4):
            step = 1 << bit
            odd = (lane // step) % 2 == 1
            later = list(groups)
            for g in range(16):
                if g & step == 0:
                    low, high = groups[g], groups[g + step]
                    later[g] = jnp.where(odd, pltpu.roll(high, step, 1), low)
                    later[g + step] = jnp.where(odd, high, pltpu.roll(low, LANES - step, 1))
            groups = later
        halves.append(jnp.concatenate(groups, axis=0))
    return jnp.concatenate(halves, axis=1)


def body(
    loop_count,
    pair_count,
    orb_hbm,
    coul_hbm,
    q_hbm,
    fit_hbm,
    screen_hbm,
    out_ref,
    orb_ref,
    coul_ref,
    q_ref,
    fit,
    screen,
    fit_own,
    mixed,
    between,
    turned,
    arrived,
    part,
    leaving,
    landed,
    orb_sem,
    coul_sem,
    q_sem,
    fit_sem,
    screen_sem,
    orb_send,
    orb_recv,
    part_send,
    part_recv,
):
    per_dev = orb_ref.shape[0]
    width, n_q, n_g = screen.shape
    rows = NV * NC // pair_count
    me = lax.axis_index("kloop")
    side = lax.axis_index("pair")
    chunks = chunks_of(width, n_q)
    chunk = width // chunks

    def fetch(index):
        span = pl.ds(index * chunk, chunk)
        return pltpu.make_async_copy(screen_hbm.at[span], screen.at[span], screen_sem.at[index])

    fit_copy = pltpu.make_async_copy(fit_hbm, fit, fit_sem)
    orb_copy = pltpu.make_async_copy(orb_hbm, orb_ref, orb_sem)
    coul_copy = pltpu.make_async_copy(coul_hbm, coul_ref, coul_sem)
    q_copy = pltpu.make_async_copy(q_hbm, q_ref, q_sem)
    for copy in (orb_copy, coul_copy, q_copy, fit_copy):
        copy.start()
    barrier = pltpu.get_barrier_semaphore()
    for shift in range(1, S + 1):
        source = lax.rem(me + shift, loop_count)
        pl.semaphore_signal(barrier, inc=1, device_id={"kloop": source}, device_id_type=MESH)
    for offset in range(1, pair_count):
        other = lax.rem(side + offset, pair_count)
        pl.semaphore_signal(barrier, inc=1, device_id={"pair": other}, device_id_type=MESH)

    pl.semaphore_wait(barrier, S + pair_count - 1)
    orb_copies = []
    for shift in range(1, S + 1):
        target = lax.rem(me - shift + loop_count, loop_count)
        orb_copies.append(
            pltpu.make_async_remote_copy(
                src_ref=orb_hbm,
                dst_ref=arrived.at[shift - 1],
                send_sem=orb_send.at[shift - 1],
                recv_sem=orb_recv.at[shift - 1],
                device_id={"kloop": target},
                device_id_type=MESH,
            )
        )
        orb_copies[-1].start()

    for copy in (fit_copy, orb_copy, coul_copy, q_copy):
        copy.wait()
    for index in range(chunks):
        fetch(index).start()
    all_weights = coul_ref[...].reshape(1, n_g)
    for index in range(pair_count):

        @pl.when(side == index)
        def _():
            own = fit[index * width : (index + 1) * width, :]
            across = own.T
            fit_own[...] = across
            weight = all_weights[:, index * width : (index + 1) * width]
            weighted = (across.astype(jnp.float32) * weight).astype(jnp.bfloat16)
            coupling = dot(weighted, own).astype(jnp.bfloat16)
            for k in range(per_dev):
                orb = orb_ref[k].astype(jnp.float32)
                turned[k] = dot(products(orb[:NV], orb[NV:]), coupling).astype(jnp.bfloat16)

    for index in range(chunks):
        fetch(index).wait()
        taken = screen[pl.ds(index * chunk, chunk)].reshape(chunk * n_q, n_g)
        start = pl.multiple_of(index * chunk * n_q, 8)
        result = dot(taken, fit[...])
        for tile in range(result.shape[1] // LANES):
            mixed[tile, pl.ds(start, chunk * n_q), :] = result[:, tile * LANES : (tile + 1) * LANES]

    for q in range(n_q):
        half = jnp.concatenate(
            [mixed[tile, pl.ds(q, width, stride=n_q), :] for tile in range(mixed.shape[0])], axis=1
        )
        between[q] = dot(fit_own[...], half.astype(jnp.bfloat16)).astype(jnp.bfloat16)

    part_copies = []
    for shift in range(1, S + 1):
        orb_copies[shift - 1].wait()
        for k in range(per_dev):
            block = (shift - 1) * per_dev + k
            row = arrived[shift - 1, k].astype(jnp.float32)
            col = orb_ref[k].astype(jnp.float32)
            q = q_ref[shift - 1, me * per_dev + k]
            cond = products(col[NV:], row[NV:])
            screened = dot_nt(cond, between[q]).astype(jnp.bfloat16)
            direct = exchange_digits(dot_nt(screened, products(col[:NV], row[:NV])))
            exchange = dot_nt(products(row[:NV], row[NV:]), turned[k])
            total = 2.0 * exchange - direct
            part[block] = total
            leaving[block] = total.astype(jnp.bfloat16)
            for offset in range(1, pair_count):
                other = lax.rem(side + offset, pair_count)
                copy = pltpu.make_async_remote_copy(
                    src_ref=leaving.at[block, pl.ds(pl.multiple_of(other * rows, rows), rows)],
                    dst_ref=landed.at[block, offset - 1],
                    send_sem=part_send.at[block, offset - 1],
                    recv_sem=part_recv.at[block, offset - 1],
                    device_id={"pair": other},
                    device_id_type=MESH,
                )
                copy.start()
                part_copies.append(copy)

    for shift in range(1, S + 1):
        for k in range(per_dev):
            block = (shift - 1) * per_dev + k
            total = part[block, pl.ds(pl.multiple_of(side * rows, rows), rows), :]
            for offset in range(1, pair_count):
                part_copies[block * (pair_count - 1) + offset - 1].wait()
                total = total + landed[block, offset - 1].astype(jnp.float32)
            out_ref[k, shift - 1] = total.astype(jnp.bfloat16)


def shards(orbitals, fitting, screen, coulomb, qindex):
    per_dev, bands, points = orbitals.shape
    pair_count = lax.axis_size("pair")
    loop_count = lax.axis_size("kloop")
    n_q, n_g, width = screen.shape
    rows = NV * NC // pair_count
    blocks = S * per_dev
    n = NV * NC
    flops = 2 * n_q * points * width * (n_g + points) + 2 * points * points * width
    flops += blocks * 2 * n * points * (points + 2 * n)
    vmem = pl.BlockSpec(memory_space=pltpu.VMEM)
    dma = pltpu.SemaphoreType.DMA
    return pl.pallas_call(
        functools.partial(body, loop_count, pair_count),
        out_shape=jax.ShapeDtypeStruct((per_dev, S, rows, n), jnp.bfloat16),
        in_specs=[
            pl.BlockSpec(memory_space=pltpu.HBM),
            pl.BlockSpec(memory_space=pltpu.HBM),
            pl.BlockSpec(memory_space=pltpu.HBM),
            pl.BlockSpec(memory_space=pltpu.HBM),
            pl.BlockSpec(memory_space=pltpu.HBM),
        ],
        out_specs=vmem,
        scratch_shapes=[
            pltpu.VMEM((per_dev, bands, points), jnp.bfloat16),
            pltpu.VMEM((n_g,), jnp.float32),
            pltpu.SMEM((S, per_dev * loop_count), jnp.int32),
            pltpu.VMEM((n_g, points), jnp.bfloat16),
            pltpu.VMEM((width, n_q, n_g), jnp.bfloat16),
            pltpu.VMEM((points, width), jnp.bfloat16),
            pltpu.VMEM((points // LANES, width * n_q, LANES), jnp.float32),
            pltpu.VMEM((n_q, points, points), jnp.bfloat16),
            pltpu.VMEM((per_dev, n, points), jnp.bfloat16),
            pltpu.VMEM((S, per_dev, bands, points), jnp.bfloat16),
            pltpu.VMEM((blocks, n, n), jnp.float32),
            pltpu.VMEM((blocks, n, n), jnp.bfloat16),
            pltpu.VMEM((blocks, max(pair_count - 1, 1), rows, n), jnp.bfloat16),
            dma,
            dma,
            dma,
            dma,
            dma((chunks_of(width, n_q),)),
            dma((S,)),
            dma((S,)),
            dma((blocks, max(pair_count - 1, 1))),
            dma((blocks, max(pair_count - 1, 1))),
        ],
        compiler_params=pltpu.CompilerParams(
            collective_id=0, has_side_effects=True, vmem_limit_bytes=64 * 1024 * 1024
        ),
        cost_estimate=pl.CostEstimate(
            flops=flops, bytes_accessed=2 * (n_q * n_g * width + points * n_g), transcendentals=0
        ),
    )(orbitals, coulomb, qindex.T, fitting.T, jnp.transpose(screen, (2, 0, 1)))


def solution(mesh):
    return jax.shard_map(
        shards,
        mesh=mesh,
        in_specs=(P("kloop", None, None), P(), P(None, None, "pair"), P(), P()),
        out_specs=P("kloop", None, "pair", None),
        check_vma=False,
    )
```

```python
import functools
import jax
import jax.numpy as jnp
from jax import lax
from jax.experimental import pallas as pl
from jax.experimental.pallas import tpu as pltpu
from jax.sharding import PartitionSpec as P

NV = 16
NC = 16
S = 2
LANES = 128
MESH = pl.DeviceIdType.MESH
NT = (((1,), (1,)), ((), ()))


def dot(left, right):
    return jnp.dot(left, right, preferred_element_type=jnp.float32)


def dot_nt(left, right):
    return lax.dot_general(left, right, NT, preferred_element_type=jnp.float32)


def products(major, minor):
    both = major[:, None, :] * minor[None, :, :]
    return both.astype(jnp.bfloat16).reshape(major.shape[0] * minor.shape[0], major.shape[1])


def chunks_of(width, n_q):
    for count in (5, 7, 4, 3, 2):
        if width % count == 0 and width // count * n_q % 16 == 0:
            return count
    return 1


def exchange_digits(value):
    lane = lax.broadcasted_iota(jnp.int32, (16, LANES), 1)
    halves = []
    for half in range(value.shape[1] // LANES):
        groups = [
            value[16 * g : 16 * g + 16, half * LANES : (half + 1) * LANES] for g in range(16)
        ]
        for bit in range(4):
            step = 1 << bit
            odd = (lane // step) % 2 == 1
            later = list(groups)
            for g in range(16):
                if g & step == 0:
                    low, high = groups[g], groups[g + step]
                    later[g] = jnp.where(odd, pltpu.roll(high, step, 1), low)
                    later[g + step] = jnp.where(odd, high, pltpu.roll(low, LANES - step, 1))
            groups = later
        halves.append(jnp.concatenate(groups, axis=0))
    return jnp.concatenate(halves, axis=1)


def body(
    loop_count,
    pair_count,
    orb_hbm,
    coul_hbm,
    q_hbm,
    fit_hbm,
    screen_hbm,
    out_ref,
    orb_ref,
    coul_ref,
    q_ref,
    fit,
    screen,
    fit_own,
    mixed,
    between,
    turned,
    arrived,
    part,
    leaving,
    landed,
    orb_sem,
    coul_sem,
    q_sem,
    fit_sem,
    screen_sem,
    orb_send,
    orb_recv,
    part_send,
    part_recv,
):
    per_dev = orb_ref.shape[0]
    width, n_q, n_g = screen.shape
    rows = NV * NC // pair_count
    me = lax.axis_index("kloop")
    side = lax.axis_index("pair")
    chunks = chunks_of(width, n_q)
    chunk = width // chunks

    def fetch(index):
        span = pl.ds(index * chunk, chunk)
        return pltpu.make_async_copy(screen_hbm.at[span], screen.at[span], screen_sem.at[index])

    fit_copy = pltpu.make_async_copy(fit_hbm, fit, fit_sem)
    orb_copy = pltpu.make_async_copy(orb_hbm, orb_ref, orb_sem)
    coul_copy = pltpu.make_async_copy(coul_hbm, coul_ref, coul_sem)
    q_copy = pltpu.make_async_copy(q_hbm, q_ref, q_sem)
    for copy in (orb_copy, coul_copy, q_copy, fit_copy):
        copy.start()
    for index in range(chunks):
        fetch(index).start()

    barrier = pltpu.get_barrier_semaphore()
    for shift in range(1, S + 1):
        source = lax.rem(me + shift, loop_count)
        pl.semaphore_signal(barrier, inc=1, device_id={"kloop": source}, device_id_type=MESH)
    for offset in range(1, pair_count):
        other = lax.rem(side + offset, pair_count)
        pl.semaphore_signal(barrier, inc=1, device_id={"pair": other}, device_id_type=MESH)

    for copy in (orb_copy, coul_copy, q_copy, fit_copy):
        copy.wait()
    all_weights = coul_ref[...].reshape(1, n_g)
    for index in range(pair_count):

        @pl.when(side == index)
        def _():
            own = fit[index * width : (index + 1) * width, :]
            across = own.T
            fit_own[...] = across
            weight = all_weights[:, index * width : (index + 1) * width]
            weighted = (across.astype(jnp.float32) * weight).astype(jnp.bfloat16)
            coupling = dot(weighted, own).astype(jnp.bfloat16)
            for k in range(per_dev):
                orb = orb_ref[k].astype(jnp.float32)
                turned[k] = dot(products(orb[:NV], orb[NV:]), coupling).astype(jnp.bfloat16)

    pl.semaphore_wait(barrier, S + pair_count - 1)
    orb_copies = []
    for shift in range(1, S + 1):
        target = lax.rem(me - shift + loop_count, loop_count)
        orb_copies.append(
            pltpu.make_async_remote_copy(
                src_ref=orb_ref,
                dst_ref=arrived.at[shift - 1],
                send_sem=orb_send.at[shift - 1],
                recv_sem=orb_recv.at[shift - 1],
                device_id={"kloop": target},
                device_id_type=MESH,
            )
        )
        orb_copies[-1].start()

    for index in range(chunks):
        fetch(index).wait()
        taken = screen[pl.ds(index * chunk, chunk)].reshape(chunk * n_q, n_g)
        start = pl.multiple_of(index * chunk * n_q, 8)
        result = dot(taken, fit[...])
        for tile in range(result.shape[1] // LANES):
            mixed[tile, pl.ds(start, chunk * n_q), :] = result[:, tile * LANES : (tile + 1) * LANES]

    for q in range(n_q):
        half = jnp.concatenate(
            [mixed[tile, pl.ds(q, width, stride=n_q), :] for tile in range(mixed.shape[0])], axis=1
        )
        between[q] = dot(fit_own[...], half.astype(jnp.bfloat16)).astype(jnp.bfloat16)

    part_copies = []
    for shift in range(1, S + 1):
        orb_copies[shift - 1].wait()
        for k in range(per_dev):
            block = (shift - 1) * per_dev + k
            row = arrived[shift - 1, k].astype(jnp.float32)
            col = orb_ref[k].astype(jnp.float32)
            q = q_ref[shift - 1, me * per_dev + k]
            cond = products(col[NV:], row[NV:])
            screened = dot_nt(cond, between[q]).astype(jnp.bfloat16)
            direct = exchange_digits(dot_nt(screened, products(col[:NV], row[:NV])))
            exchange = dot_nt(products(row[:NV], row[NV:]), turned[k])
            total = 2.0 * exchange - direct
            part[block] = total
            leaving[block] = total.astype(jnp.bfloat16)
            for offset in range(1, pair_count):
                other = lax.rem(side + offset, pair_count)
                copy = pltpu.make_async_remote_copy(
                    src_ref=leaving.at[block, pl.ds(pl.multiple_of(other * rows, rows), rows)],
                    dst_ref=landed.at[block, offset - 1],
                    send_sem=part_send.at[block, offset - 1],
                    recv_sem=part_recv.at[block, offset - 1],
                    device_id={"pair": other},
                    device_id_type=MESH,
                )
                copy.start()
                part_copies.append(copy)

    for shift in range(1, S + 1):
        for k in range(per_dev):
            block = (shift - 1) * per_dev + k
            total = part[block, pl.ds(pl.multiple_of(side * rows, rows), rows), :]
            for offset in range(1, pair_count):
                part_copies[block * (pair_count - 1) + offset - 1].wait()
                total = total + landed[block, offset - 1].astype(jnp.float32)
            out_ref[k, shift - 1] = total.astype(jnp.bfloat16)


def shards(orbitals, fitting, screen, coulomb, qindex):
    per_dev, bands, points = orbitals.shape
    pair_count = lax.axis_size("pair")
    loop_count = lax.axis_size("kloop")
    n_q, n_g, width = screen.shape
    rows = NV * NC // pair_count
    blocks = S * per_dev
    n = NV * NC
    flops = 2 * n_q * points * width * (n_g + points) + 2 * points * points * width
    flops += blocks * 2 * n * points * (points + 2 * n)
    vmem = pl.BlockSpec(memory_space=pltpu.VMEM)
    dma = pltpu.SemaphoreType.DMA
    return pl.pallas_call(
        functools.partial(body, loop_count, pair_count),
        out_shape=jax.ShapeDtypeStruct((per_dev, S, rows, n), jnp.bfloat16),
        in_specs=[
            pl.BlockSpec(memory_space=pltpu.HBM),
            pl.BlockSpec(memory_space=pltpu.HBM),
            pl.BlockSpec(memory_space=pltpu.HBM),
            pl.BlockSpec(memory_space=pltpu.HBM),
            pl.BlockSpec(memory_space=pltpu.HBM),
        ],
        out_specs=vmem,
        scratch_shapes=[
            pltpu.VMEM((per_dev, bands, points), jnp.bfloat16),
            pltpu.VMEM((n_g,), jnp.float32),
            pltpu.SMEM((S, per_dev * loop_count), jnp.int32),
            pltpu.VMEM((n_g, points), jnp.bfloat16),
            pltpu.VMEM((width, n_q, n_g), jnp.bfloat16),
            pltpu.VMEM((points, width), jnp.bfloat16),
            pltpu.VMEM((points // LANES, width * n_q, LANES), jnp.float32),
            pltpu.VMEM((n_q, points, points), jnp.bfloat16),
            pltpu.VMEM((per_dev, n, points), jnp.bfloat16),
            pltpu.VMEM((S, per_dev, bands, points), jnp.bfloat16),
            pltpu.VMEM((blocks, n, n), jnp.float32),
            pltpu.VMEM((blocks, n, n), jnp.bfloat16),
            pltpu.VMEM((blocks, max(pair_count - 1, 1), rows, n), jnp.bfloat16),
            dma,
            dma,
            dma,
            dma,
            dma((chunks_of(width, n_q),)),
            dma((S,)),
            dma((S,)),
            dma((blocks, max(pair_count - 1, 1))),
            dma((blocks, max(pair_count - 1, 1))),
        ],
        compiler_params=pltpu.CompilerParams(
            collective_id=0, has_side_effects=True, vmem_limit_bytes=64 * 1024 * 1024
        ),
        cost_estimate=pl.CostEstimate(
            flops=flops, bytes_accessed=2 * (n_q * n_g * width + points * n_g), transcendentals=0
        ),
    )(orbitals, coulomb, qindex.T, fitting.T, jnp.transpose(screen, (2, 0, 1)))


def solution(mesh):
    return jax.shard_map(
        shards,
        mesh=mesh,
        in_specs=(P("kloop", None, None), P(), P(None, None, "pair"), P(), P()),
        out_specs=P("kloop", None, "pair", None),
        check_vma=False,
    )
```

```python
import functools
import jax
import jax.numpy as jnp
from jax import lax
from jax.experimental import pallas as pl
from jax.experimental.pallas import tpu as pltpu
from jax.sharding import PartitionSpec as P

NV = 16
NC = 16
S = 2
LANES = 128
MESH = pl.DeviceIdType.MESH
NT = (((1,), (1,)), ((), ()))


def dot(left, right):
    return jnp.dot(left, right, preferred_element_type=jnp.float32)


def dot_nt(left, right):
    return lax.dot_general(left, right, NT, preferred_element_type=jnp.float32)


def products(major, minor):
    both = major[:, None, :] * minor[None, :, :]
    return both.astype(jnp.bfloat16).reshape(major.shape[0] * minor.shape[0], major.shape[1])


def chunks_of(width, n_q):
    for count in (5, 7, 4, 3, 2):
        if width % count == 0 and width // count * n_q % 16 == 0:
            return count
    return 1


def exchange_digits(value):
    lane = lax.broadcasted_iota(jnp.int32, (16, LANES), 1)
    halves = []
    for half in range(value.shape[1] // LANES):
        groups = [
            value[16 * g : 16 * g + 16, half * LANES : (half + 1) * LANES] for g in range(16)
        ]
        for bit in range(4):
            step = 1 << bit
            odd = (lane // step) % 2 == 1
            later = list(groups)
            for g in range(16):
                if g & step == 0:
                    low, high = groups[g], groups[g + step]
                    later[g] = jnp.where(odd, pltpu.roll(high, step, 1), low)
                    later[g + step] = jnp.where(odd, high, pltpu.roll(low, LANES - step, 1))
            groups = later
        halves.append(jnp.concatenate(groups, axis=0))
    return jnp.concatenate(halves, axis=1)


def body(
    loop_count,
    pair_count,
    orb_hbm,
    coul_hbm,
    q_hbm,
    fit_hbm,
    screen_hbm,
    out_ref,
    orb_ref,
    coul_ref,
    q_ref,
    fit,
    screen,
    fit_own,
    mixed,
    between,
    turned,
    arrived,
    part,
    leaving,
    landed,
    orb_sem,
    coul_sem,
    q_sem,
    fit_sem,
    screen_sem,
    orb_send,
    orb_recv,
    part_send,
    part_recv,
):
    per_dev = orb_ref.shape[0]
    width, n_q, n_g = screen.shape
    rows = NV * NC // pair_count
    me = lax.axis_index("kloop")
    side = lax.axis_index("pair")
    chunks = chunks_of(width, n_q)
    chunk = width // chunks

    def fetch(index):
        span = pl.ds(index * chunk, chunk)
        return pltpu.make_async_copy(screen_hbm.at[span], screen.at[span], screen_sem.at[index])

    fit_copy = pltpu.make_async_copy(fit_hbm, fit, fit_sem)
    orb_copy = pltpu.make_async_copy(orb_hbm, orb_ref, orb_sem)
    coul_copy = pltpu.make_async_copy(coul_hbm, coul_ref, coul_sem)
    q_copy = pltpu.make_async_copy(q_hbm, q_ref, q_sem)
    for copy in (orb_copy, coul_copy, q_copy, fit_copy):
        copy.start()
    for index in range(chunks):
        fetch(index).start()

    barrier = pltpu.get_barrier_semaphore()
    for shift in range(1, S + 1):
        source = lax.rem(me + shift, loop_count)
        pl.semaphore_signal(barrier, inc=1, device_id={"kloop": source}, device_id_type=MESH)
    for offset in range(1, pair_count):
        other = lax.rem(side + offset, pair_count)
        pl.semaphore_signal(barrier, inc=1, device_id={"pair": other}, device_id_type=MESH)

    for copy in (orb_copy, coul_copy, q_copy, fit_copy):
        copy.wait()
    pl.semaphore_wait(barrier, S + pair_count - 1)
    orb_copies = []
    for shift in range(1, S + 1):
        target = lax.rem(me - shift + loop_count, loop_count)
        orb_copies.append(
            pltpu.make_async_remote_copy(
                src_ref=orb_ref,
                dst_ref=arrived.at[shift - 1],
                send_sem=orb_send.at[shift - 1],
                recv_sem=orb_recv.at[shift - 1],
                device_id={"kloop": target},
                device_id_type=MESH,
            )
        )
        orb_copies[-1].start()

    all_weights = coul_ref[...].reshape(1, n_g)
    for index in range(pair_count):

        @pl.when(side == index)
        def _():
            own = fit[index * width : (index + 1) * width, :]
            across = own.T
            fit_own[...] = across
            weight = all_weights[:, index * width : (index + 1) * width]
            weighted = (across.astype(jnp.float32) * weight).astype(jnp.bfloat16)
            coupling = dot(weighted, own).astype(jnp.bfloat16)
            for k in range(per_dev):
                orb = orb_ref[k].astype(jnp.float32)
                turned[k] = dot(products(orb[:NV], orb[NV:]), coupling).astype(jnp.bfloat16)

    for index in range(chunks):
        fetch(index).wait()
        taken = screen[pl.ds(index * chunk, chunk)].reshape(chunk * n_q, n_g)
        start = pl.multiple_of(index * chunk * n_q, 8)
        result = dot(taken, fit[...])
        for tile in range(result.shape[1] // LANES):
            mixed[tile, pl.ds(start, chunk * n_q), :] = result[:, tile * LANES : (tile + 1) * LANES]

    for q in range(n_q):
        half = jnp.concatenate(
            [mixed[tile, pl.ds(q, width, stride=n_q), :] for tile in range(mixed.shape[0])], axis=1
        )
        between[q] = dot(fit_own[...], half.astype(jnp.bfloat16)).astype(jnp.bfloat16)

    part_copies = []
    for shift in range(1, S + 1):
        orb_copies[shift - 1].wait()
        for k in range(per_dev):
            block = (shift - 1) * per_dev + k
            row = arrived[shift - 1, k].astype(jnp.float32)
            col = orb_ref[k].astype(jnp.float32)
            q = q_ref[shift - 1, me * per_dev + k]
            cond = products(col[NV:], row[NV:])
            screened = dot_nt(cond, between[q]).astype(jnp.bfloat16)
            direct = exchange_digits(dot_nt(screened, products(col[:NV], row[:NV])))
            exchange = dot_nt(products(row[:NV], row[NV:]), turned[k])
            total = 2.0 * exchange - direct
            part[block] = total
            leaving[block] = total.astype(jnp.bfloat16)
            for offset in range(1, pair_count):
                other = lax.rem(side + offset, pair_count)
                copy = pltpu.make_async_remote_copy(
                    src_ref=leaving.at[block, pl.ds(pl.multiple_of(other * rows, rows), rows)],
                    dst_ref=landed.at[block, offset - 1],
                    send_sem=part_send.at[block, offset - 1],
                    recv_sem=part_recv.at[block, offset - 1],
                    device_id={"pair": other},
                    device_id_type=MESH,
                )
                copy.start()
                part_copies.append(copy)

    for shift in range(1, S + 1):
        for k in range(per_dev):
            block = (shift - 1) * per_dev + k
            total = part[block, pl.ds(pl.multiple_of(side * rows, rows), rows), :]
            for offset in range(1, pair_count):
                part_copies[block * (pair_count - 1) + offset - 1].wait()
                total = total + landed[block, offset - 1].astype(jnp.float32)
            out_ref[k, shift - 1] = total.astype(jnp.bfloat16)


def shards(orbitals, fitting, screen, coulomb, qindex):
    per_dev, bands, points = orbitals.shape
    pair_count = lax.axis_size("pair")
    loop_count = lax.axis_size("kloop")
    n_q, n_g, width = screen.shape
    rows = NV * NC // pair_count
    blocks = S * per_dev
    n = NV * NC
    flops = 2 * n_q * points * width * (n_g + points) + 2 * points * points * width
    flops += blocks * 2 * n * points * (points + 2 * n)
    vmem = pl.BlockSpec(memory_space=pltpu.VMEM)
    dma = pltpu.SemaphoreType.DMA
    return pl.pallas_call(
        functools.partial(body, loop_count, pair_count),
        out_shape=jax.ShapeDtypeStruct((per_dev, S, rows, n), jnp.bfloat16),
        in_specs=[
            pl.BlockSpec(memory_space=pltpu.HBM),
            pl.BlockSpec(memory_space=pltpu.HBM),
            pl.BlockSpec(memory_space=pltpu.HBM),
            pl.BlockSpec(memory_space=pltpu.HBM),
            pl.BlockSpec(memory_space=pltpu.HBM),
        ],
        out_specs=vmem,
        scratch_shapes=[
            pltpu.VMEM((per_dev, bands, points), jnp.bfloat16),
            pltpu.VMEM((n_g,), jnp.float32),
            pltpu.SMEM((S, per_dev * loop_count), jnp.int32),
            pltpu.VMEM((n_g, points), jnp.bfloat16),
            pltpu.VMEM((width, n_q, n_g), jnp.bfloat16),
            pltpu.VMEM((points, width), jnp.bfloat16),
            pltpu.VMEM((points // LANES, width * n_q, LANES), jnp.float32),
            pltpu.VMEM((n_q, points, points), jnp.bfloat16),
            pltpu.VMEM((per_dev, n, points), jnp.bfloat16),
            pltpu.VMEM((S, per_dev, bands, points), jnp.bfloat16),
            pltpu.VMEM((blocks, n, n), jnp.float32),
            pltpu.VMEM((blocks, n, n), jnp.bfloat16),
            pltpu.VMEM((blocks, max(pair_count - 1, 1), rows, n), jnp.bfloat16),
            dma,
            dma,
            dma,
            dma,
            dma((chunks_of(width, n_q),)),
            dma((S,)),
            dma((S,)),
            dma((blocks, max(pair_count - 1, 1))),
            dma((blocks, max(pair_count - 1, 1))),
        ],
        compiler_params=pltpu.CompilerParams(
            collective_id=0, has_side_effects=True, vmem_limit_bytes=64 * 1024 * 1024
        ),
        cost_estimate=pl.CostEstimate(
            flops=flops, bytes_accessed=2 * (n_q * n_g * width + points * n_g), transcendentals=0
        ),
    )(orbitals, coulomb, qindex.T, fitting.T, jnp.transpose(screen, (2, 0, 1)))


def solution(mesh):
    return jax.shard_map(
        shards,
        mesh=mesh,
        in_specs=(P("kloop", None, None), P(), P(None, None, "pair"), P(), P()),
        out_specs=P("kloop", None, "pair", None),
        check_vma=False,
    )
```
